32 devices in a mesh: gx: 4 (over x, core), gy: 4 (over z), gz: 2 (over y).
Axes of the slice: x: 2, y: 2, z: 4, core: 2. Of those that a mesh axis runs over, the one named last changes fastest.
Arguments:
- field: float32 [64, 32, 512], P('gx', 'gz', 'gy'), may hold values from -6 to 6
Outputs:
- coefficients: float32 [64, 32, 512], P('gx', 'gz', 'gy')
The draws below stay inside these ranges and needn't reach their ends.
All inputs are finite; a program needn't handle non-finite values.
Results may differ from the reference program's by a relative error of at most 0.00002.
Values sent between devices are 32-bit elements; how exact they have to be, the bound alone decides.
A program may use at most 64 MiB of HBM per device.

```python
import jax
import jax.numpy as jnp
from jax import lax

NX = 64
NY = 512
NZ = 32


def levels(rng, shape, cuts, low, high):
    loudness = 1.0
    for position, blocks in cuts:
        steps = jax.random.uniform(jax.random.fold_in(jax.random.fold_in(rng, 6), position), (blocks,), jnp.float32, low / len(cuts), high / len(cuts))
        loudness = loudness * jnp.repeat(jnp.exp(steps), shape[position] // blocks).reshape((-1,) + (1,) * (len(shape) - 1 - position))
    return loudness


def noise(stream_key, dims, deviation, limit, pieces=(), held_as=jnp.bfloat16):
    loudness = levels(stream_key, dims, pieces, -0.22, 0.18) if pieces else 1.0
    values = jax.random.normal(stream_key, dims, jnp.float32) * deviation * loudness
    return jnp.minimum(jnp.maximum(values, -limit), limit).astype(held_as)


def setup_inputs(seed: int = 0) -> dict:
    key_list = jax.random.split(jax.random.key(seed), 2)
    return {
        "field": noise(key_list[0], (NX, NZ, NY), 1.0, 6.0, ((0, 4), (1, 2), (2, 4)), jnp.float32),
    }


ALPHA = -1.586134342
BETA = -0.05298011854
GAMMA = 0.8829110762
DELTA = 0.4435068522
ZETA = 1.149604398


def piece(array, start, stop, dim):
    return lax.slice_in_dim(array, start, stop, axis=dim)


def lift_padded(padded, dim):
    total = padded.shape[dim]
    half = total // 2
    shape = padded.shape[:dim] + (half, 2) + padded.shape[dim + 1:]
    pairs = padded.reshape(shape)
    even = lax.index_in_dim(pairs, 0, dim + 1, keepdims=False)
    odd = lax.index_in_dim(pairs, 1, dim + 1, keepdims=False)
    odd_one = piece(odd, 0, half - 1, dim) + ALPHA * (piece(even, 0, half - 1, dim) + piece(even, 1, half, dim))
    even_two = piece(even, 1, half - 1, dim) + BETA * (piece(odd_one, 0, half - 2, dim) + piece(odd_one, 1, half - 1, dim))
    odd_three = piece(odd_one, 1, half - 2, dim) + GAMMA * (piece(even_two, 0, half - 3, dim) + piece(even_two, 1, half - 2, dim))
    even_four = piece(even_two, 1, half - 3, dim) + DELTA * (piece(odd_three, 0, half - 4, dim) + piece(odd_three, 1, half - 3, dim))
    lowpass = even_four * ZETA
    highpass = piece(odd_three, 1, half - 3, dim) / ZETA
    joined = jnp.stack([lowpass, highpass], axis=dim + 1)
    out_shape = padded.shape[:dim] + (total - 8,) + padded.shape[dim + 1:]
    return joined.reshape(out_shape)


def lift_axis(array, dim):
    widths = [(0, 0)] * array.ndim
    widths[dim] = (4, 4)
    return lift_padded(jnp.pad(array, widths, mode="reflect"), dim)


def lift_three(array):
    for dim in range(3):
        array = lift_axis(array, dim)
    return array


def reference(field):
    level_one = lift_three(field)
    coarse = level_one[::2, ::2, ::2]
    level_two = lift_three(coarse)
    return level_one.at[::2, ::2, ::2].set(level_two)
```

```python
import functools

import jax
import jax.numpy as jnp
from jax import lax
from jax.experimental import pallas as pl
from jax.experimental.pallas import tpu as pltpu
from jax.sharding import PartitionSpec as P

ALPHA = -1.586134342
BETA = -0.05298011854
GAMMA = 0.8829110762
DELTA = 0.4435068522
ZETA = 1.149604398
MESH = pl.DeviceIdType.MESH

FAR_LOW, FAR_HIGH = 12, 9
NEAR_LOW, NEAR_HIGH = 4, 3


def replaced(array, at, source, condition):
    entry = jnp.where(condition, array[source : source + 1], array[at : at + 1])
    parts = [array[:at]] if at else []
    parts.append(entry)
    if at + 1 < array.shape[0]:
        parts.append(array[at + 1 :])
    return jnp.concatenate(parts, axis=0)


def neighbours(array):
    return array[:-1] + array[1:]


def lift(even, odd, low, half, first, last):
    at = low + half
    odd = odd + ALPHA * neighbours(replaced(even, at, at - 1, last))
    even = even[1:-1] + BETA * neighbours(replaced(odd, low - 1, low, first))
    at = at - 1
    odd = odd[1:-1] + GAMMA * neighbours(replaced(even, at, at - 1, last))
    even = even[1:-1] + DELTA * neighbours(replaced(odd, low - 2, low - 1, first))
    return even * ZETA, odd * (1.0 / ZETA)


def split(cells):
    count = cells.shape[0]
    pairs = cells[: count // 2 * 2].reshape((count // 2, 2) + cells.shape[1:])
    even, odd = pairs[:, 0], pairs[:, 1]
    if count % 2:
        even = jnp.concatenate([even, cells[count - 1 :]], axis=0)
    return even, odd


def joined(even, odd):
    count = even.shape[0]
    return jnp.stack([even, odd], axis=1).reshape((2 * count,) + even.shape[1:])


def one_level(cells, low, first, last, half):
    even, odd = split(cells)
    even, odd = lift(even, odd, low // 2, half, first, last)
    begin = low // 2 - 1
    return even, odd[begin : begin + half]


def lift_lanes(main, halo, stride, lane, first, last):
    width = main.shape[-1]
    phase = lane % (2 * stride)
    is_even, is_odd = phase == 0, phase == stride
    low_edge, high_edge = lane < stride, lane >= width - stride
    low_end = (lane == 0) & first
    high_end = (lane == width - stride) & last
    for coefficient, mask in (
        (ALPHA, is_odd), (BETA, is_even), (GAMMA, is_odd), (DELTA, is_even),
    ):
        weight = jnp.where(mask, coefficient, 0.0)
        main_low, halo_low = pltpu.roll(main, stride, 1), pltpu.roll(halo, stride, 1)
        main_high, halo_high = (
            pltpu.roll(main, width - stride, 1), pltpu.roll(halo, width - stride, 1),
        )
        left = jnp.where(low_edge, halo_low, main_low)
        right = jnp.where(high_edge, halo_high, main_high)
        around_halo = jnp.where(low_edge, main_low, halo_low) + jnp.where(
            high_edge, main_high, halo_high
        )
        around = jnp.where(low_end, right, left) + jnp.where(high_end, left, right)
        main = main + weight * around
        halo = halo + weight * around_halo
    scale = jnp.where(is_even, ZETA, 1.0 / ZETA)
    return main * scale, halo * scale


def packed(tiles, low, lane):
    width = tiles[0].shape[-1]
    room = 2 * low
    per = width // room
    packs = []
    for start in range(0, len(tiles), per):
        pack = None
        for place, tile in enumerate(tiles[start : start + per]):
            moved = pltpu.roll(tile, (place * room + low) % width, 1)
            pack = moved if pack is None else jnp.where(lane // room == place, moved, pack)
        packs.append(pack)
    return packs


def unpacked(packs, low, count):
    width = packs[0].shape[-1]
    room = 2 * low
    per = width // room
    return [
        pltpu.roll(packs[t // per], (2 * width - (t % per) * room - low) % width, 1)
        for t in range(count)
    ]


def kernel(sizes, field, out, wide, near, far, edges, from_low, from_high, load_sem, send_sem, recv_sem):
    nx, nz, ny = field.shape
    place = {axis: lax.axis_index(axis) for axis in sizes}
    first = {axis: place[axis] == 0 for axis in sizes}
    last = {axis: place[axis] == sizes[axis] - 1 for axis in sizes}

    load = pltpu.make_async_copy(field, wide.at[pl.ds(FAR_LOW, nx)], load_sem)
    load.start()

    barrier = pltpu.get_barrier_semaphore()
    arrivals = 0
    for axis in sizes:
        for end, step in ((first, -1), (last, 1)):
            arrivals = arrivals + jnp.where(end[axis], 0, 1)

            @pl.when(jnp.logical_not(end[axis]))
            def _():
                pl.semaphore_signal(
                    barrier, inc=1, device_id={axis: place[axis] + step}, device_id_type=MESH
                )

    pl.semaphore_wait(barrier, arrivals)

    def shift(slot, axis, step, source, target):
        copy = pltpu.make_async_remote_copy(
            src_ref=source,
            dst_ref=target,
            send_sem=send_sem.at[slot],
            recv_sem=recv_sem.at[slot],
            device_id={axis: place[axis] + step},
            device_id_type=MESH,
        )
        sends = jnp.logical_not(last[axis] if step > 0 else first[axis])
        receives = jnp.logical_not(first[axis] if step > 0 else last[axis])
        pl.when(sends)(copy.start)
        return (lambda: pl.when(receives)(copy.wait_recv)), (lambda: pl.when(sends)(copy.wait_send))

    sent = []

    def exchange(*moves):
        waits = []
        for move in moves:
            arrived, left = shift(*move)
            waits.append(arrived)
            sent.append(left)
        for wait in waits:
            wait()

    moves = (
        (0, "gx", 1, field.at[pl.ds(nx - FAR_LOW, FAR_LOW)], wide.at[pl.ds(0, FAR_LOW)]),
        (1, "gx", -1, field.at[pl.ds(0, FAR_HIGH)], wide.at[pl.ds(FAR_LOW + nx, FAR_HIGH)]),
    )
    exchange(*moves)
    load.wait()
    ends = first["gx"], last["gx"]
    coarse, high = one_level(wide[...], FAR_LOW, *ends, nx // 2)
    begin = FAR_LOW // 2 - 2
    low = coarse[begin : begin + nx // 2]
    coarse = joined(*one_level(coarse, NEAR_LOW, *ends, nx // 4))

    half = nx // 2
    near[NEAR_LOW : NEAR_LOW + nz, :half] = jnp.swapaxes(low, 0, 1)
    near[NEAR_LOW : NEAR_LOW + nz, half:] = jnp.swapaxes(high, 0, 1)
    far[FAR_LOW : FAR_LOW + nz] = jnp.swapaxes(coarse, 0, 1)
    exchange(
        (2, "gz", 1, near.at[pl.ds(nz, NEAR_LOW)], near.at[pl.ds(0, NEAR_LOW)]),
        (3, "gz", -1, near.at[pl.ds(NEAR_LOW, NEAR_HIGH)], near.at[pl.ds(NEAR_LOW + nz, NEAR_HIGH)]),
        (4, "gz", 1, far.at[pl.ds(nz, FAR_LOW)], far.at[pl.ds(0, FAR_LOW)]),
        (5, "gz", -1, far.at[pl.ds(FAR_LOW, FAR_HIGH)], far.at[pl.ds(FAR_LOW + nz, FAR_HIGH)]),
    )
    ends = first["gz"], last["gz"]
    fine = joined(*one_level(near[...], NEAR_LOW, *ends, nz // 2))
    coarse, _ = one_level(far[...], FAR_LOW, *ends, nz // 2)
    coarse = joined(*one_level(coarse, NEAR_LOW, *ends, nz // 4))

    lane = lax.broadcasted_iota(jnp.int32, (half, ny), 1)
    fine_tiles = [fine[z, p * half : (p + 1) * half] for z in range(nz) for p in range(2)]
    coarse_tiles = [coarse[z] for z in range(nz // 2)]
    fine_packs = packed(fine_tiles, NEAR_LOW, lane)
    coarse_packs = packed(coarse_tiles, 16, lane)
    split_at = len(fine_packs)
    for i, pack in enumerate(fine_packs + coarse_packs):
        edges[i] = pack
    exchange((6, "gy", 1, edges, from_low), (7, "gy", -1, edges, from_high))
    ends = first["gy"], last["gy"]
    beside = [
        jnp.where(lane % (2 * NEAR_LOW) < NEAR_LOW, from_low[i], from_high[i]) for i in range(split_at)
    ]
    halo = unpacked(beside, NEAR_LOW, len(fine_tiles))
    lane_at = lax.broadcasted_iota(jnp.int32, (1, ny), 1)
    fine, _ = lift_lanes(
        jnp.concatenate(fine_tiles, axis=0), jnp.concatenate(halo, axis=0), 1, lane_at, *ends
    )
    beside = [
        jnp.where(lane % 32 < 16, from_low[i], from_high[i])
        for i in range(split_at, split_at + len(coarse_packs))
    ]
    halo = unpacked(beside, 16, len(coarse_tiles))
    pair = lift_lanes(
        jnp.concatenate(coarse_tiles, axis=0), jnp.concatenate(halo, axis=0), 1, lane_at, *ends
    )
    coarse, _ = lift_lanes(*pair, 2, lane_at, *ends)

    fine = fine.reshape(nz // 2, 2, 2, half, ny)
    coarse = coarse.reshape(nz // 2, half, ny)
    merged = jnp.where(lane % 2 == 0, coarse, fine[:, 0, 0])
    low = joined(merged, fine[:, 1, 0])
    high = joined(fine[:, 0, 1], fine[:, 1, 1])
    out[...] = joined(jnp.swapaxes(low, 0, 1), jnp.swapaxes(high, 0, 1))
    for wait in sent:
        wait()


def on_device(sizes, field):
    nx, nz, ny = field.shape
    half = nx // 2
    count = nz * 2 * 2 * NEAR_LOW // ny + nz // 2 * 32 // ny
    return pl.pallas_call(
        functools.partial(kernel, sizes),
        out_shape=jax.ShapeDtypeStruct(field.shape, field.dtype),
        in_specs=[pl.BlockSpec(memory_space=pl.ANY)],
        out_specs=pl.BlockSpec(memory_space=pltpu.VMEM),
        scratch_shapes=[
            pltpu.VMEM((FAR_LOW + nx + FAR_HIGH, nz, ny), jnp.float32),
            pltpu.VMEM((NEAR_LOW + nz + NEAR_HIGH, nx, ny), jnp.float32),
            pltpu.VMEM((FAR_LOW + nz + FAR_HIGH, half, ny), jnp.float32),
            pltpu.VMEM((count, half, ny), jnp.float32),
            pltpu.VMEM((count, half, ny), jnp.float32),
            pltpu.VMEM((count, half, ny), jnp.float32),
            pltpu.SemaphoreType.DMA,
            pltpu.SemaphoreType.DMA((8,)),
            pltpu.SemaphoreType.DMA((8,)),
        ],
        compiler_params=pltpu.CompilerParams(
            collective_id=0, has_side_effects=True, vmem_limit_bytes=32 * 1024 * 1024
        ),
        cost_estimate=pl.CostEstimate(flops=4_000_000, bytes_accessed=1_000_000, transcendentals=0),
    )(field)


def solution(mesh):
    sizes = {axis: mesh.shape[axis] for axis in ("gx", "gz", "gy")}
    placed = P("gx", "gz", "gy")
    return jax.shard_map(
        functools.partial(on_device, sizes),
        mesh=mesh, in_specs=(placed,), out_specs=placed, check_vma=False,
    )
```

```python
import functools

import jax
import jax.numpy as jnp
from jax import lax
from jax.experimental import pallas as pl
from jax.experimental.pallas import tpu as pltpu
from jax.sharding import PartitionSpec as P

ALPHA = -1.586134342
BETA = -0.05298011854
GAMMA = 0.8829110762
DELTA = 0.4435068522
ZETA = 1.149604398
MESH = pl.DeviceIdType.MESH

FAR_LOW, FAR_HIGH = 12, 9
NEAR_LOW, NEAR_HIGH = 4, 3
NEAR_ROOM, FAR_ROOM = 8, 32


def replaced(array, at, source, condition):
    entry = jnp.where(condition, array[source : source + 1], array[at : at + 1])
    parts = [array[:at]] if at else []
    parts.append(entry)
    if at + 1 < array.shape[0]:
        parts.append(array[at + 1 :])
    return jnp.concatenate(parts, axis=0)


def neighbours(array):
    return array[:-1] + array[1:]


def lift(even, odd, low, half, first, last):
    at = low + half
    odd = odd + ALPHA * neighbours(replaced(even, at, at - 1, last))
    even = even[1:-1] + BETA * neighbours(replaced(odd, low - 1, low, first))
    at = at - 1
    odd = odd[1:-1] + GAMMA * neighbours(replaced(even, at, at - 1, last))
    even = even[1:-1] + DELTA * neighbours(replaced(odd, low - 2, low - 1, first))
    return even * ZETA, odd * (1.0 / ZETA)


def split(cells):
    count = cells.shape[0]
    pairs = cells[: count // 2 * 2].reshape((count // 2, 2) + cells.shape[1:])
    even, odd = pairs[:, 0], pairs[:, 1]
    if count % 2:
        even = jnp.concatenate([even, cells[count - 1 :]], axis=0)
    return even, odd


def joined(even, odd):
    count = even.shape[0]
    return jnp.stack([even, odd], axis=1).reshape((2 * count,) + even.shape[1:])


def one_level(even, odd, low, first, last, half):
    even, odd = lift(even, odd, low // 2, half, first, last)
    begin = low // 2 - 1
    return even, odd[begin : begin + half]


def lift_lanes(main, halo, stride, lane, first, last):
    width = main.shape[-1]
    phase = lane % (2 * stride)
    is_even, is_odd = phase == 0, phase == stride
    low_edge, high_edge = lane < stride, lane >= width - stride
    low_end = (lane == 0) & first
    high_end = (lane == width - stride) & last
    for coefficient, mask in (
        (ALPHA, is_odd), (BETA, is_even), (GAMMA, is_odd), (DELTA, is_even),
    ):
        weight = jnp.where(mask, coefficient, 0.0)
        main_low, halo_low = pltpu.roll(main, stride, 1), pltpu.roll(halo, stride, 1)
        main_high, halo_high = (
            pltpu.roll(main, width - stride, 1), pltpu.roll(halo, width - stride, 1),
        )
        left = jnp.where(low_edge, halo_low, main_low)
        right = jnp.where(high_edge, halo_high, main_high)
        around_halo = jnp.where(low_edge, main_low, halo_low) + jnp.where(
            high_edge, main_high, halo_high
        )
        around = jnp.where(low_end, right, left) + jnp.where(high_end, left, right)
        main = main + weight * around
        halo = halo + weight * around_halo
    scale = jnp.where(is_even, ZETA, 1.0 / ZETA)
    return main * scale, halo * scale


def edge_pack(near, far, lane):
    width = lane.shape[-1]
    half = width // 2
    pack = None
    for slot in range(2):
        start = slot * half
        part = pltpu.roll(far[slot], start + NEAR_ROOM * 2 + FAR_ROOM // 2, 1)
        for p in range(2):
            at = start + NEAR_ROOM * p
            moved = pltpu.roll(near[slot][p], at + NEAR_ROOM // 2, 1)
            part = jnp.where((lane >= at) & (lane < at + NEAR_ROOM), moved, part)
        pack = part if pack is None else jnp.where(lane >= half, part, pack)
    return pack


def from_low_side(lane):
    at = lane % (lane.shape[-1] // 2)
    beside_near = (at < 2 * NEAR_ROOM) & (at % NEAR_ROOM < NEAR_ROOM // 2)
    return beside_near | ((at >= 2 * NEAR_ROOM) & (at < 2 * NEAR_ROOM + FAR_ROOM // 2))


def kernel(sizes, field, out, wide, near, far, edges, from_low, from_high, load_sem, send_sem, recv_sem):
    nx, nz, ny = field.shape
    place = {axis: lax.axis_index(axis) for axis in sizes}
    first = {axis: place[axis] == 0 for axis in sizes}
    last = {axis: place[axis] == sizes[axis] - 1 for axis in sizes}

    ways = [{axis: step} for axis in sizes for step in (-1, 1)]
    ways += [{"gz": up, "gy": step} for up in (-1, 1) for step in (-1, 1)]

    def exists(way):
        there = None
        for axis, step in way.items():
            inside = jnp.logical_not(last[axis] if step > 0 else first[axis])
            there = inside if there is None else there & inside
        return there

    def device(way):
        return {axis: place[axis] + step for axis, step in way.items()}

    barrier = pltpu.get_barrier_semaphore()
    arrivals = 0
    for way in ways:
        there = exists(way)
        arrivals = arrivals + jnp.where(there, 1, 0)

        @pl.when(there)
        def _():
            pl.semaphore_signal(barrier, inc=1, device_id=device(way), device_id_type=MESH)

    load = pltpu.make_async_copy(field, wide.at[pl.ds(FAR_LOW, nx)], load_sem)
    load.start()
    pl.semaphore_wait(barrier, arrivals)

    def shift(slot, way, source, target):
        copy = pltpu.make_async_remote_copy(
            src_ref=source,
            dst_ref=target,
            send_sem=send_sem.at[slot],
            recv_sem=recv_sem.at[slot],
            device_id=device(way),
            device_id_type=MESH,
        )
        sends = exists(way)
        receives = exists({axis: -step for axis, step in way.items()})
        pl.when(sends)(copy.start)
        return (lambda: pl.when(receives)(copy.wait_recv)), (lambda: pl.when(sends)(copy.wait_send))

    sent = []

    def exchange(*moves):
        waits = {}
        for move in moves:
            arrived, left = shift(*move)
            waits[move[0]] = arrived
            sent.append(left)
        return lambda *slots: [waits[slot]() for slot in slots]

    arrived = exchange(
        (0, {"gx": 1}, field.at[pl.ds(nx - FAR_LOW, FAR_LOW)], wide.at[pl.ds(0, FAR_LOW)]),
        (1, {"gx": -1}, field.at[pl.ds(0, FAR_HIGH)], wide.at[pl.ds(FAR_LOW + nx, FAR_HIGH)]),
    )
    arrived(0, 1)
    load.wait()
    ends = first["gx"], last["gx"]
    coarse, high = one_level(*split(wide[...]), FAR_LOW, *ends, nx // 2)
    begin = FAR_LOW // 2 - 2
    low = coarse[begin : begin + nx // 2]
    coarse = joined(*one_level(*split(coarse), NEAR_LOW, *ends, nx // 4))

    half, pairs = nx // 2, nz // 2
    lane = lax.broadcasted_iota(jnp.int32, (half, ny), 1)
    low, high, coarse = (jnp.swapaxes(part, 0, 1) for part in (low, high, coarse))
    near[NEAR_LOW : NEAR_LOW + nz, :half] = low
    near[NEAR_LOW : NEAR_LOW + nz, half:] = high
    far[FAR_LOW : FAR_LOW + nz] = coarse
    for pair in range(pairs):
        layers = (2 * pair, 2 * pair + 1)
        edges[pair] = edge_pack([(low[z], high[z]) for z in layers], [coarse[z] for z in layers], lane)
    moves = [
        (2, {"gz": 1}, near.at[pl.ds(nz, NEAR_LOW)], near.at[pl.ds(0, NEAR_LOW)]),
        (3, {"gz": -1}, near.at[pl.ds(NEAR_LOW, NEAR_HIGH)], near.at[pl.ds(NEAR_LOW + nz, NEAR_HIGH)]),
        (4, {"gz": 1}, far.at[pl.ds(nz, FAR_LOW)], far.at[pl.ds(0, FAR_LOW)]),
        (5, {"gz": -1}, far.at[pl.ds(FAR_LOW, FAR_HIGH)], far.at[pl.ds(FAR_LOW + nz, FAR_HIGH)]),
    ]
    below, above = FAR_LOW // 2, (FAR_HIGH + 1) // 2
    for slot, step, target in ((6, 1, from_low), (9, -1, from_high)):
        moves += [
            (slot, {"gy": step}, edges, target.at[pl.ds(below, pairs)]),
            (slot + 1, {"gz": 1, "gy": step}, edges.at[pl.ds(pairs - below, below)], target.at[pl.ds(0, below)]),
            (slot + 2, {"gz": -1, "gy": step}, edges.at[pl.ds(0, above)], target.at[pl.ds(below + pairs, above)]),
        ]
    arrived = exchange(*moves)

    ends = first["gz"], last["gz"]
    arrived(2, 3)
    fine = joined(*one_level(*split(near[...]), NEAR_LOW, *ends, pairs))
    arrived(4, 5)
    coarse, _ = one_level(*split(far[...]), FAR_LOW, *ends, pairs)
    coarse = joined(*one_level(*split(coarse), NEAR_LOW, *ends, nz // 4))
    arrived(*range(6, 12))
    beside = jnp.where(from_low_side(lane), from_low[...], from_high[...])
    turned = pltpu.roll(beside[:-1].reshape(-1, ny), ny // 2, 1).reshape(-1, half, ny)
    around, around_high = one_level(beside, turned, FAR_LOW, *ends, pairs)
    begin = FAR_LOW // 2 - 2
    around_fine = joined(around[begin : begin + pairs], around_high)
    around_coarse = joined(*one_level(*split(around), NEAR_LOW, *ends, nz // 4))

    fine = fine.reshape(nz, 2, half, ny)
    around_fine = around_fine.reshape(-1, ny)
    halo = jnp.stack(
        [
            pltpu.roll(around_fine, ny - NEAR_ROOM * p - NEAR_ROOM // 2, 1).reshape(nz, half, ny)
            for p in range(2)
        ],
        axis=1,
    )
    ends = first["gy"], last["gy"]
    lane_at = lax.broadcasted_iota(jnp.int32, (1, ny), 1)
    fine, _ = lift_lanes(fine.reshape(-1, ny), halo.reshape(-1, ny), 1, lane_at, *ends)
    halo = pltpu.roll(around_coarse.reshape(-1, ny), ny - 2 * NEAR_ROOM - FAR_ROOM // 2, 1)
    coarse, halo = lift_lanes(coarse.reshape(-1, ny), halo, 1, lane_at, *ends)
    coarse, _ = lift_lanes(coarse, halo, 2, lane_at, *ends)

    fine = fine.reshape(nz // 2, 2, 2, half, ny)
    coarse = coarse.reshape(nz // 2, half, ny)
    merged = jnp.where(lane % 2 == 0, coarse, fine[:, 0, 0])
    low = joined(merged, fine[:, 1, 0])
    high = joined(fine[:, 0, 1], fine[:, 1, 1])
    out[...] = joined(jnp.swapaxes(low, 0, 1), jnp.swapaxes(high, 0, 1))
    for wait in sent:
        wait()


def on_device(sizes, field):
    nx, nz, ny = field.shape
    half = nx // 2
    pairs = nz // 2
    around = FAR_LOW // 2 + pairs + (FAR_HIGH + 1) // 2
    return pl.pallas_call(
        functools.partial(kernel, sizes),
        out_shape=jax.ShapeDtypeStruct(field.shape, field.dtype),
        in_specs=[pl.BlockSpec(memory_space=pltpu.HBM)],
        out_specs=pl.BlockSpec(memory_space=pltpu.VMEM),
        scratch_shapes=[
            pltpu.VMEM((FAR_LOW + nx + FAR_HIGH, nz, ny), jnp.float32),
            pltpu.VMEM((NEAR_LOW + nz + NEAR_HIGH, nx, ny), jnp.float32),
            pltpu.VMEM((FAR_LOW + nz + FAR_HIGH, half, ny), jnp.float32),
            pltpu.VMEM((pairs, half, ny), jnp.float32),
            pltpu.VMEM((around, half, ny), jnp.float32),
            pltpu.VMEM((around, half, ny), jnp.float32),
            pltpu.SemaphoreType.DMA,
            pltpu.SemaphoreType.DMA((12,)),
            pltpu.SemaphoreType.DMA((12,)),
        ],
        compiler_params=pltpu.CompilerParams(
            collective_id=0, has_side_effects=True, vmem_limit_bytes=32 * 1024 * 1024
        ),
        cost_estimate=pl.CostEstimate(flops=4_000_000, bytes_accessed=1_000_000, transcendentals=0),
    )(field)


def solution(mesh):
    sizes = {axis: mesh.shape[axis] for axis in ("gx", "gz", "gy")}
    placed = P("gx", "gz", "gy")
    return jax.shard_map(
        functools.partial(on_device, sizes),
        mesh=mesh, in_specs=(placed,), out_specs=placed, check_vma=False,
    )
```

```python
import functools

import jax
import jax.numpy as jnp
import numpy as np
from jax import lax
from jax.experimental import pallas as pl
from jax.experimental.pallas import tpu as pltpu
from jax.sharding import PartitionSpec as P

ALPHA = -1.586134342
BETA = -0.05298011854
GAMMA = 0.8829110762
DELTA = 0.4435068522
ZETA = 1.149604398
MESH = pl.DeviceIdType.MESH

FAR_LOW, FAR_HIGH = 12, 9
NEAR_LOW, NEAR_HIGH = 4, 3
NEAR_ROOM, FAR_ROOM = 8, 32


def replaced(array, at, source, condition):
    entry = jnp.where(condition, array[source : source + 1], array[at : at + 1])
    parts = [array[:at]] if at else []
    parts.append(entry)
    if at + 1 < array.shape[0]:
        parts.append(array[at + 1 :])
    return jnp.concatenate(parts, axis=0)


def neighbours(array):
    return array[:-1] + array[1:]


def lift(even, odd, low, half, first, last):
    at = low + half
    odd = odd + ALPHA * neighbours(replaced(even, at, at - 1, last))
    even = even[1:-1] + BETA * neighbours(replaced(odd, low - 1, low, first))
    at = at - 1
    odd = odd[1:-1] + GAMMA * neighbours(replaced(even, at, at - 1, last))
    even = even[1:-1] + DELTA * neighbours(replaced(odd, low - 2, low - 1, first))
    return even * ZETA, odd * (1.0 / ZETA)


def split(cells):
    count = cells.shape[0]
    pairs = cells[: count // 2 * 2].reshape((count // 2, 2) + cells.shape[1:])
    even, odd = pairs[:, 0], pairs[:, 1]
    if count % 2:
        even = jnp.concatenate([even, cells[count - 1 :]], axis=0)
    return even, odd


def joined(even, odd):
    count = even.shape[0]
    return jnp.stack([even, odd], axis=1).reshape((2 * count,) + even.shape[1:])


def one_level(even, odd, low, first, last, half):
    even, odd = lift(even, odd, low // 2, half, first, last)
    begin = low // 2 - 1
    return even, odd[begin : begin + half]


def lift_rows(cells):
    even, odd = cells[0::2], cells[1::2]
    count = min(len(even) - 1, len(odd))
    even, odd = even[: count + 1], odd[:count]
    odd = odd + ALPHA * neighbours(even)
    even = even[1:-1] + BETA * neighbours(odd)
    odd = odd[1:-1] + GAMMA * neighbours(even)
    even = even[1:-1] + DELTA * neighbours(odd)
    return even * ZETA, odd[1:] / ZETA


def mirrored_rows(cells, low, count, first, last):
    cells = cells.copy()
    if first:
        for k in range(1, low + 1):
            cells[low - k] = cells[low + k]
    if last:
        for k in range(1, len(cells) - low - count + 1):
            cells[low + count - 1 + k] = cells[low + count - 1 - k]
    return cells


def y_matrices(ny):
    cases = []
    for case in range(4):
        first, last = case % 2 == 1, case >= 2
        matrices = np.zeros((5, ny, ny))
        low, high = FAR_LOW, FAR_LOW
        inputs = np.eye(low + ny + high)
        cells = mirrored_rows(inputs, low, ny, first, last)
        even, odd = lift_rows(cells)
        begin = low // 2 - 2
        one = np.zeros((ny, len(inputs)))
        one[0::2] = even[begin : begin + ny // 2]
        one[1::2] = odd[begin : begin + ny // 2]
        coarse = mirrored_rows(even, begin, ny // 2, first, last)
        even, odd = lift_rows(coarse)
        two = np.zeros((ny, len(inputs)))
        two[0::4] = even[begin // 2 - 2 :][: ny // 4]
        two[2::4] = odd[begin // 2 - 2 :][: ny // 4]
        one, two = one.T, two.T
        matrices[0], matrices[3] = one[low : low + ny], two[low : low + ny]
        room = NEAR_ROOM // 2
        for p in range(2):
            at = NEAR_ROOM * p
            matrices[1 + p, at : at + room] = one[low - room : low]
            matrices[1 + p, at + room : at + 2 * room] = one[low + ny : low + ny + room]
        at, room = 2 * NEAR_ROOM, FAR_ROOM // 2
        matrices[4, at + room - low : at + room] = two[:low]
        matrices[4, at + room : at + room + high] = two[low + ny :]
        cases.append(matrices)
    return np.stack(cases).astype(np.float32)


def edge_pack(near, far, lane):
    width = lane.shape[-1]
    half = width // 2
    pack = None
    for slot in range(2):
        start = slot * half
        part = pltpu.roll(far[slot], start + NEAR_ROOM * 2 + FAR_ROOM // 2, 1)
        for p in range(2):
            at = start + NEAR_ROOM * p
            moved = pltpu.roll(near[slot][p], at + NEAR_ROOM // 2, 1)
            part = jnp.where((lane >= at) & (lane < at + NEAR_ROOM), moved, part)
        pack = part if pack is None else jnp.where(lane >= half, part, pack)
    return pack


def packed_sides(lane):
    at = lane % (lane.shape[-1] // 2)
    is_near, is_far = at < 2 * NEAR_ROOM, (at >= 2 * NEAR_ROOM) & (at < 2 * NEAR_ROOM + FAR_ROOM)
    near_low = at % NEAR_ROOM < NEAR_ROOM // 2
    far_low = at < 2 * NEAR_ROOM + FAR_ROOM // 2
    return (is_near & near_low) | (is_far & far_low), (is_near & ~near_low) | (is_far & ~far_low)


def kernel(sizes, field, matrices, out, wide, near, far, edges, from_low, from_high, held, load_sem, send_sem, recv_sem):
    nx, nz, ny = field.shape
    place = {axis: lax.axis_index(axis) for axis in sizes}
    first = {axis: place[axis] == 0 for axis in sizes}
    last = {axis: place[axis] == sizes[axis] - 1 for axis in sizes}

    ways = [{axis: step} for axis in sizes for step in (-1, 1)]
    ways += [{"gz": up, "gy": step} for up in (-1, 1) for step in (-1, 1)]

    def exists(way):
        there = None
        for axis, step in way.items():
            inside = jnp.logical_not(last[axis] if step > 0 else first[axis])
            there = inside if there is None else there & inside
        return there

    def device(way):
        return {axis: place[axis] + step for axis, step in way.items()}

    barrier = pltpu.get_barrier_semaphore()
    arrivals = 0
    for way in ways:
        there = exists(way)
        arrivals = arrivals + jnp.where(there, 1, 0)

        @pl.when(there)
        def _():
            pl.semaphore_signal(barrier, inc=1, device_id=device(way), device_id_type=MESH)

    load = pltpu.make_async_copy(field, wide.at[pl.ds(FAR_LOW, nx)], load_sem.at[0])
    load.start()
    case = jnp.where(first["gy"], 1, 0) + jnp.where(last["gy"], 2, 0)
    fetch = pltpu.make_async_copy(matrices.at[case], held, load_sem.at[1])
    fetch.start()
    load.wait()
    pl.semaphore_wait(barrier, arrivals)

    def shift(slot, way, source, target):
        copy = pltpu.make_async_remote_copy(
            src_ref=source,
            dst_ref=target,
            send_sem=send_sem.at[slot],
            recv_sem=recv_sem.at[slot],
            device_id=device(way),
            device_id_type=MESH,
        )
        sends = exists(way)
        receives = exists({axis: -step for axis, step in way.items()})
        pl.when(sends)(copy.start)
        return (lambda: pl.when(receives)(copy.wait_recv)), (lambda: pl.when(sends)(copy.wait_send))

    sent = []

    def exchange(*moves):
        waits = {}
        for move in moves:
            arrived, left = shift(*move)
            waits[move[0]] = arrived
            sent.append(left)
        return lambda *slots: [waits[slot]() for slot in slots]

    arrived = exchange(
        (0, {"gx": 1}, wide.at[pl.ds(nx, FAR_LOW)], wide.at[pl.ds(0, FAR_LOW)]),
        (1, {"gx": -1}, wide.at[pl.ds(FAR_LOW, FAR_HIGH)], wide.at[pl.ds(FAR_LOW + nx, FAR_HIGH)]),
    )
    arrived(0, 1)
    ends = first["gx"], last["gx"]
    coarse, high = one_level(*split(wide[...]), FAR_LOW, *ends, nx // 2)
    begin = FAR_LOW // 2 - 2
    low = coarse[begin : begin + nx // 2]
    coarse = joined(*one_level(*split(coarse), NEAR_LOW, *ends, nx // 4))

    half, pairs = nx // 2, nz // 2
    lane = lax.broadcasted_iota(jnp.int32, (half, ny), 1)
    low, high, coarse = (jnp.swapaxes(part, 0, 1) for part in (low, high, coarse))
    near[NEAR_LOW : NEAR_LOW + nz, :half] = low
    near[NEAR_LOW : NEAR_LOW + nz, half:] = high
    far[FAR_LOW : FAR_LOW + nz] = coarse
    for pair in range(pairs):
        layers = (2 * pair, 2 * pair + 1)
        edges[pair] = edge_pack([(low[z], high[z]) for z in layers], [coarse[z] for z in layers], lane)
    moves = [
        (2, {"gz": 1}, near.at[pl.ds(nz, NEAR_LOW)], near.at[pl.ds(0, NEAR_LOW)]),
        (3, {"gz": -1}, near.at[pl.ds(NEAR_LOW, NEAR_HIGH)], near.at[pl.ds(NEAR_LOW + nz, NEAR_HIGH)]),
        (4, {"gz": 1}, far.at[pl.ds(nz, FAR_LOW)], far.at[pl.ds(0, FAR_LOW)]),
        (5, {"gz": -1}, far.at[pl.ds(FAR_LOW, FAR_HIGH)], far.at[pl.ds(FAR_LOW + nz, FAR_HIGH)]),
    ]
    below, above = FAR_LOW // 2, (FAR_HIGH + 1) // 2
    for slot, step, target in ((6, 1, from_low), (9, -1, from_high)):
        moves += [
            (slot, {"gy": step}, edges, target.at[pl.ds(below, pairs)]),
            (slot + 1, {"gz": 1, "gy": step}, edges.at[pl.ds(pairs - below, below)], target.at[pl.ds(0, below)]),
            (slot + 2, {"gz": -1, "gy": step}, edges.at[pl.ds(0, above)], target.at[pl.ds(below + pairs, above)]),
        ]
    arrived = exchange(*moves)

    ends = first["gz"], last["gz"]
    arrived(2, 3)
    fine = joined(*one_level(*split(near[...]), NEAR_LOW, *ends, pairs))
    arrived(4, 5)
    coarse, _ = one_level(*split(far[...]), FAR_LOW, *ends, pairs)
    coarse = joined(*one_level(*split(coarse), NEAR_LOW, *ends, nz // 4))
    arrived(*range(6, 12))
    low_side, high_side = packed_sides(lane)
    low_side, high_side = low_side & ~first["gy"], high_side & ~last["gy"]
    beside = jnp.where(low_side, from_low[...], jnp.where(high_side, from_high[...], 0.0))
    turned = pltpu.roll(beside[:-1].reshape(-1, ny), ny // 2, 1).reshape(-1, half, ny)
    around, around_high = one_level(beside, turned, FAR_LOW, *ends, pairs)
    begin = FAR_LOW // 2 - 2
    around_fine = joined(around[begin : begin + pairs], around_high)
    around_coarse = joined(*one_level(*split(around), NEAR_LOW, *ends, nz // 4))

    fetch.wait()

    def times(cells, edge_cells, cell_matrix, edge_matrix):
        cells = jnp.concatenate([cells.reshape(-1, ny), edge_cells.reshape(-1, ny)], axis=1)
        matrix = jnp.concatenate([held[cell_matrix], held[edge_matrix]], axis=0)
        return jnp.dot(
            cells, matrix, precision=lax.Precision.HIGHEST, preferred_element_type=jnp.float32
        ).reshape(-1, half, ny)

    fine = [
        times(fine[:, p * half : (p + 1) * half], around_fine, 0, 1 + p).reshape(pairs, 2, half, ny)
        for p in range(2)
    ]
    coarse = times(coarse, around_coarse, 3, 4)

    low = joined(jnp.where(lane % 2 == 0, coarse, fine[0][:, 0]), fine[0][:, 1])
    high = fine[1].reshape(nz, half, ny)
    out[...] = joined(jnp.swapaxes(low, 0, 1), jnp.swapaxes(high, 0, 1))
    for wait in sent:
        wait()


def on_device(sizes, field):
    nx, nz, ny = field.shape
    half = nx // 2
    pairs = nz // 2
    around = FAR_LOW // 2 + pairs + (FAR_HIGH + 1) // 2
    return pl.pallas_call(
        functools.partial(kernel, sizes),
        out_shape=jax.ShapeDtypeStruct(field.shape, field.dtype),
        in_specs=[pl.BlockSpec(memory_space=pltpu.HBM)] * 2,
        out_specs=pl.BlockSpec(memory_space=pltpu.VMEM),
        scratch_shapes=[
            pltpu.VMEM((FAR_LOW + nx + FAR_HIGH, nz, ny), jnp.float32),
            pltpu.VMEM((NEAR_LOW + nz + NEAR_HIGH, nx, ny), jnp.float32),
            pltpu.VMEM((FAR_LOW + nz + FAR_HIGH, half, ny), jnp.float32),
            pltpu.VMEM((pairs, half, ny), jnp.float32),
            pltpu.VMEM((around, half, ny), jnp.float32),
            pltpu.VMEM((around, half, ny), jnp.float32),
            pltpu.VMEM((5, ny, ny), jnp.float32),
            pltpu.SemaphoreType.DMA((2,)),
            pltpu.SemaphoreType.DMA((12,)),
            pltpu.SemaphoreType.DMA((12,)),
        ],
        compiler_params=pltpu.CompilerParams(
            collective_id=0, has_side_effects=True, vmem_limit_bytes=63488 * 1024
        ),
        cost_estimate=pl.CostEstimate(flops=4_000_000, bytes_accessed=1_000_000, transcendentals=0),
    )(field, jnp.asarray(y_matrices(ny)))


def solution(mesh):
    sizes = {axis: mesh.shape[axis] for axis in ("gx", "gz", "gy")}
    placed = P("gx", "gz", "gy")
    return jax.shard_map(
        functools.partial(on_device, sizes),
        mesh=mesh, in_specs=(placed,), out_specs=placed, check_vma=False,
    )
```
